32 devices in a mesh: dp: 32 (over z, y, x, core).
Axes of the slice: x: 2, y: 2, z: 4, core: 2. Of those that a mesh axis runs over, the one named last changes fastest.
Arguments:
- tokens: bfloat16 [65536, 768], P('dp'), may hold values from -6 to 6
- params: bfloat16 [2, 3765344], P(None, 'dp')
- segments: int32 [65536], P('dp'), may hold values from -1 to 65535, as said below
- cotangent: bfloat16 [65536, 768], P('dp'), may hold values from -6 to 6
Outputs:
- out_tokens: bfloat16 [65536, 768], P('dp')
- grad_tokens: float32 [65536, 768], P('dp')
- grad_params: float32 [2, 3765344], P(None, 'dp')
The draws below stay inside these ranges and needn't reach their ends.
Inputs may be any that keep to these rules, and one draw needn't show every extreme that they name: `segments`: within each device's block of 1024 slots (one micro-batch), the slots of one packed sequence stand together and share a number that no other sequence has; numbers never fall within a block; unused slots (-1) all stand at a block's end; some block holds one sequence of all 1024 slots.
All inputs are finite; a program needn't handle non-finite values.
Results may differ from the reference program's by a relative error of at most 0.0087.
Values may be sent and summed in bfloat16 or wider, within the bound.
A program may use at most 576 MiB of HBM per device.

```python
import math
import jax
import jax.numpy as jnp
from jax import lax

D = 768
INNER = 1536
HEADDIM = 64
STATE = 128
KERNEL = 4
GROUP = 256
MB_TOK = 1024
LAYERS = 2
HEADS = 24
CONVCH = 1792
PROJ = 3352
PADDED = 3765344
TOKENS = 65536


def draw_params(key, part):
    key = jax.random.fold_in(key, 7)
    gauss_key, uniform_key = jax.random.split(key)
    full_shape = (LAYERS, PADDED)
    gaussian = jax.random.normal(gauss_key, full_shape, jnp.float32)
    uniform_draw = jax.random.uniform(uniform_key, full_shape, jnp.float32)
    position = jnp.broadcast_to(jnp.arange(PADDED)[None, :], full_shape)
    edge_one = D
    edge_two = edge_one + D * PROJ
    edge_three = edge_two + KERNEL * CONVCH
    edge_four = edge_three + CONVCH
    edge_five = edge_four + HEADS
    edge_six = edge_five + HEADS
    edge_seven = edge_six + HEADS
    edge_eight = edge_seven + INNER
    edge_nine = edge_eight + INNER * D
    step_init = jnp.exp(math.log(0.001) + uniform_draw * math.log(100.0))
    step_init_bias = step_init + jnp.log(-jnp.expm1(-step_init))
    gain_values = 1.0 + 0.4 * (uniform_draw - 0.5)
    values = jnp.select([position < edge_one, position < edge_two, position < edge_three, position < edge_four, position < edge_five, position < edge_six, position < edge_seven, position < edge_eight, position < edge_nine], [gain_values, gaussian * D ** (-0.5), gaussian * 0.5, gaussian * 0.2, step_init_bias, jnp.log(1.0 + 15.0 * uniform_draw), 0.5 + uniform_draw, gain_values, gaussian * INNER ** (-0.5)], gaussian * 0.02)
    return values.astype(jnp.bfloat16)


def draw_segments(key, part):
    key = jax.random.fold_in(key, 13)
    live_key, full_key, start_key = jax.random.split(key, 3)
    buffers = TOKENS // MB_TOK
    lengths = jax.random.randint(live_key, (buffers,), MB_TOK // 2, MB_TOK + 1)
    chosen = jax.random.randint(full_key, (), 0, buffers)
    buffer_ids = jnp.arange(buffers)
    lengths = jnp.where(buffer_ids == chosen, MB_TOK, lengths)
    places = jnp.arange(MB_TOK)
    starts = jax.random.randint(start_key, (buffers, MB_TOK), 0, max(MB_TOK // 4, 2)) == 0
    starts = starts & (places[None, :] > 0) & (buffer_ids[:, None] != chosen)
    live_slots = places[None, :] < lengths[:, None]
    starts = starts & live_slots
    local_ids = jnp.cumsum(starts.astype(jnp.int32), axis=1)
    total_starts = jnp.sum(starts.astype(jnp.int32), axis=1)
    numbers = buffer_ids[:, None] * MB_TOK + (MB_TOK - 1) - (total_starts[:, None] - local_ids)
    numbers = jnp.where(live_slots, numbers, -1)
    return numbers.reshape(TOKENS).astype(jnp.int32)


def shard_levels(rng, extent, cuts, least, high):
    gain = 1.0
    for axis_at, parts in cuts:
        draws = jax.random.uniform(jax.random.fold_in(jax.random.fold_in(rng, 6), axis_at), (parts,), jnp.float32, least / len(cuts), high / len(cuts))
        gain = gain * jnp.repeat(jnp.exp(draws), extent[axis_at] // parts).reshape((-1,) + (1,) * (len(extent) - 1 - axis_at))
    return gain


def bell_draw(key, dims, scale, bound, shards=(), kind=jnp.bfloat16):
    entries = jax.random.normal(key, dims, jnp.float32) * scale
    if len(shards) > 0:
        entries = shard_levels(key, dims, shards, -0.22, 0.18) * entries
    return jnp.clip(entries, min=-bound, max=bound).astype(kind)


def setup_inputs(seed: int = 0) -> dict:
    key_list = jax.random.split(jax.random.key(seed), 5)
    tokens = bell_draw(key_list[0], (TOKENS, D), 1.0, 6.0, ((0, 32),))
    params = draw_params(jax.random.fold_in(key_list[4], 71), 0)
    segments = draw_segments(jax.random.fold_in(key_list[4], 71), 0)
    cotangent = bell_draw(key_list[3], (TOKENS, D), 1.0, 6.0, ((0, 32),))
    return dict(tokens=tokens, params=params, segments=segments, cotangent=cotangent)


@jax.custom_vjp
def low(v):
    return lax.optimization_barrier(v.astype(jnp.bfloat16)).astype(jnp.float32)

@jax.custom_vjp
def low_back(v):
    return v

def low_keep(v):
    return (low(v), None)

def low_pass(kept, grad):
    return (grad,)

def back_keep(v):
    return (v, None)

def back_low(kept, grad):
    return (low(grad),)
low.defvjp(low_keep, low_pass)
low_back.defvjp(back_keep, back_low)
highest = lax.Precision.HIGHEST

def layout_shapes():
    return [(D,), (D, PROJ), (KERNEL, CONVCH), (CONVCH,), (HEADS,), (HEADS,), (HEADS,), (INNER,), (INNER, D)]

def unpack(flat_weights):
    pieces = []
    offset = 0
    for piece_shape in layout_shapes():
        amount = math.prod(piece_shape)
        pieces.append(flat_weights[offset:offset + amount].reshape(piece_shape))
        offset = offset + amount
    return pieces

def rms_scale(values):
    return values * lax.rsqrt(lax.optimization_barrier(jnp.mean(values * values, axis=-1, keepdims=True)) + 1e-05)

def group_step(state_in, block):
    feature_block, inject_block, readout_block, step_block, decay_block, segment_block, before_segment = block
    length = segment_block.shape[0]
    cumulated = jnp.cumsum(decay_block, axis=0)
    heads_cumulated = cumulated.T
    spread = heads_cumulated[:, :, None] - heads_cumulated[:, None, :]
    causal = (jnp.arange(length)[:, None] >= jnp.arange(length)[None, :]) & (segment_block[:, None] == segment_block[None, :])
    within = jnp.exp(jnp.where(causal[None], spread, -1e+30))
    scores = jnp.dot(readout_block, inject_block.T, precision=highest)
    mixing = within * scores[None] * step_block.T[:, None, :]
    inside = jnp.einsum('hts,shp->thp', mixing, feature_block, precision=highest)
    carried = (segment_block == before_segment).astype(jnp.float32)[:, None] * jnp.exp(cumulated)
    outside = jnp.einsum('tn,hpn->thp', readout_block, state_in, precision=highest) * carried[:, :, None]
    final_segment = segment_block[length - 1]
    tail_weight = jnp.exp(cumulated[length - 1][None, :] - cumulated) * step_block * (segment_block == final_segment).astype(jnp.float32)[:, None]
    kept_share = jnp.exp(cumulated[length - 1]) * (final_segment == before_segment).astype(jnp.float32)
    fresh_state = jnp.einsum('sh,shp,sn->hpn', tail_weight, feature_block, inject_block, precision=highest)
    return (state_in * kept_share[:, None, None] + fresh_state, inside + outside)

def mixer_core(projected, conv_weight, conv_bias, step_bias, decay_log, skip_gain, out_gain, segment):
    length = projected.shape[0]
    gate_part = projected[:, :INNER]
    conv_in = projected[:, INNER:INNER + CONVCH]
    step_raw = projected[:, INNER + CONVCH:]
    prior_segment = jnp.concatenate([jnp.full((KERNEL - 1,), -2, jnp.int32), segment.astype(jnp.int32)])
    padded = jnp.concatenate([jnp.zeros((KERNEL - 1, CONVCH), jnp.float32), conv_in])
    summed = jnp.zeros_like(conv_in) + conv_bias
    for tap_index in range(KERNEL):
        same_doc = (prior_segment[tap_index:tap_index + length] == segment).astype(jnp.float32)[:, None]
        summed = summed + conv_weight[tap_index] * padded[tap_index:tap_index + length] * same_doc
    activated = jax.nn.silu(summed)
    features = activated[:, :INNER]
    inject = activated[:, INNER:INNER + STATE]
    readout = activated[:, INNER + STATE:]
    step_size = jax.nn.softplus(step_raw + step_bias)
    log_decay = -jnp.exp(decay_log) * step_size
    blocks = length // GROUP
    earlier = jnp.concatenate([jnp.full((1,), -2, jnp.int32), segment[:-1].astype(jnp.int32)])
    scanned = (features.reshape(blocks, GROUP, HEADS, HEADDIM), inject.reshape(blocks, GROUP, STATE), readout.reshape(blocks, GROUP, STATE), step_size.reshape(blocks, GROUP, HEADS), log_decay.reshape(blocks, GROUP, HEADS), segment.reshape(blocks, GROUP), earlier.reshape(blocks, GROUP)[:, 0])
    state_zero = jnp.zeros((HEADS, HEADDIM, STATE), jnp.float32)
    final_state, mixed_heads = lax.scan(jax.checkpoint(group_step), state_zero, scanned)
    mixed_heads = mixed_heads.reshape(length, HEADS, HEADDIM) + skip_gain[None, :, None] * features.reshape(length, HEADS, HEADDIM)
    gated = mixed_heads.reshape(length, INNER) * jax.nn.silu(gate_part)
    return rms_scale(gated) * out_gain

def block_stack(params, stream, segment):
    live_rows = (segment >= 0).astype(jnp.float32)[:, None]
    for layer_index in range(LAYERS):
        in_gain, in_weight, conv_weight, conv_bias, step_bias, decay_log, skip_gain, out_gain, out_weight = unpack(params[layer_index])
        normed = low(rms_scale(stream) * in_gain)
        projected = low_back(jnp.dot(normed, in_weight, precision=highest))
        mixer_out = low(mixer_core(projected, conv_weight, conv_bias, step_bias, decay_log, skip_gain, out_gain, segment))
        stream = stream + low_back(jnp.dot(mixer_out, out_weight, precision=highest) * live_rows)
    return stream

def reference(tokens, params, segments, cotangent):
    buffers = TOKENS // MB_TOK
    segment_rows = segments.reshape(buffers, MB_TOK)

    def forward(weights, inputs):

        def one_buffer(buffer_pair):
            return block_stack(weights, buffer_pair[0], buffer_pair[1])
        return lax.map(jax.checkpoint(one_buffer), (inputs.reshape(buffers, MB_TOK, D), segment_rows))
    outputs, pullback = jax.vjp(forward, params.astype(jnp.float32), tokens.astype(jnp.float32))
    grad_params, grad_tokens = pullback(cotangent.astype(jnp.float32).reshape(buffers, MB_TOK, D))
    return (outputs.reshape(TOKENS, D).astype(jnp.bfloat16), grad_tokens.reshape(TOKENS, D), grad_params)
```

```python
import math

import jax
import jax.numpy as jnp
from jax import lax
from jax.experimental import pallas as pl
from jax.experimental.pallas import tpu as pltpu
from jax.sharding import PartitionSpec as P

D = 768
INNER = 1536
HEADDIM = 64
STATE = 128
KERNEL = 4
MB_TOK = 1024
LAYERS = 2
HEADS = 24
CONVCH = 1792
PROJ = 3352
PARAMS = 3765320

LANES = 128
CHUNK = 128
CHUNKS = MB_TOK // CHUNK
PAIRS = HEADS // 2
PROJ_PAD = INNER + CONVCH + LANES
STEP_AT = INNER + CONVCH
TILES = CONVCH // LANES
EDGE = 8
F32 = jnp.float32
BF16 = jnp.bfloat16
highest = lax.Precision.HIGHEST


def tile(index):
    return slice(index * LANES, (index + 1) * LANES)


def dot(left, right, left_dim=1, right_dim=0):
    return lax.dot_general(
        left, right, (((left_dim,), (right_dim,)), ((), ())), preferred_element_type=F32
    )


def exact_dot(left, right):
    return jnp.dot(left, right, preferred_element_type=F32, precision=highest)


def sigmoid(values):
    return 1.0 / (1.0 + jnp.exp(-values))


def softplus(values):
    return jnp.maximum(values, 0.0) + jnp.log1p(jnp.exp(-jnp.abs(values)))


def halves(first, second):
    lane = lax.broadcasted_iota(jnp.int32, (1, LANES), 1)
    return jnp.where(lane < HEADDIM, first, second)


def spread_column(values, index):
    return jnp.broadcast_to(values[:, index : index + 1], (CHUNK, LANES))


def conv_tile(proj_ref, shift_ref, conv_ref, mask, index):
    at = slice(INNER + index * LANES, INNER + (index + 1) * LANES)
    lanes = tile(index)
    total = conv_ref[4:5, lanes] + conv_ref[3:4, lanes] * proj_ref[:, at]
    for back in range(1, KERNEL):
        shifted = shift_ref[EDGE - back : EDGE - back + CHUNK, lanes]
        total = total + conv_ref[3 - back : 4 - back, lanes] * shifted * mask[:, back - 1 : back]
    return total


def load_shift(proj_ref, prev_ref, shift_ref):
    shift_ref[0:EDGE, :] = prev_ref[:, INNER:STEP_AT]
    shift_ref[EDGE : EDGE + CHUNK, :] = proj_ref[:, INNER:STEP_AT]


def decays(proj_ref, head_ref):
    raw = proj_ref[:, STEP_AT:PROJ_PAD] + head_ref[0:1, :]
    step = softplus(raw)
    log_decay = -head_ref[1:2, :] * step
    rows = lax.broadcasted_iota(jnp.int32, (CHUNK, CHUNK), 0)
    cols = lax.broadcasted_iota(jnp.int32, (CHUNK, CHUNK), 1)
    lower = (rows >= cols).astype(F32)
    cumulated = exact_dot(lower, log_decay)
    return raw, step, log_decay, cumulated, rows, cols


def pair_decay(cumulated, turned, bias_twice, first):
    wide_a = spread_column(cumulated, first)
    wide_b = spread_column(cumulated, first + 1)
    row = jnp.concatenate([turned[first : first + 1, :], turned[first + 1 : first + 2, :]], axis=1)
    within = jnp.exp(jnp.concatenate([wide_a, wide_b], axis=1) - row + bias_twice)
    return within, halves(wide_a, wide_b)


def stack_pair(values):
    zero = jnp.zeros_like(values)
    return jnp.concatenate([halves(values, zero), halves(zero, values)], axis=0)


def pair_row(row, first):
    return halves(row[:, first : first + 1], row[:, first + 1 : first + 2])


def forward_kernel(
    proj_ref, prev_ref, mask_ref, seg_col_ref, seg_row_ref, conv_ref, head_ref, wide_ref,
    out_ref, mixed_ref, kept_ref, state_ref, shift_ref, gated_ref,
):
    @pl.when(pl.program_id(1) == 0)
    def _():
        state_ref[...] = jnp.zeros_like(state_ref)

    load_shift(proj_ref, prev_ref, shift_ref)
    mask = mask_ref[...]
    raw, step, log_decay, cumulated, rows, cols = decays(proj_ref, head_ref)
    turned = cumulated.T
    last = cumulated[CHUNK - 1 : CHUNK, :]
    keep_row = jnp.exp(last) * mask[CHUNK - 1 : CHUNK, 5:6]
    same = (rows >= cols) & (seg_col_ref[...] == seg_row_ref[0])
    bias = jnp.where(same, 0.0, -1e30)
    bias_twice = jnp.concatenate([bias, bias], axis=1)
    summed = conv_tile(proj_ref, shift_ref, conv_ref, mask, PAIRS)
    inject = (summed * sigmoid(summed)).astype(BF16)
    summed = conv_tile(proj_ref, shift_ref, conv_ref, mask, PAIRS + 1)
    readout = (summed * sigmoid(summed)).astype(BF16)
    scores = dot(readout, inject, 1, 1)
    scores_twice = jnp.concatenate([scores, scores], axis=1)
    square = jnp.zeros((CHUNK, 1), F32)
    for pair in range(PAIRS):
        first = 2 * pair
        lanes = tile(pair)
        summed = conv_tile(proj_ref, shift_ref, conv_ref, mask, pair)
        feature = summed * sigmoid(summed)
        stepped = feature * halves(spread_column(step, first), spread_column(step, first + 1))
        within, wide = pair_decay(cumulated, turned, bias_twice, first)
        mixing = (within * scores_twice).astype(BF16)
        mixed = dot(mixing, stack_pair(stepped.astype(BF16)))
        state = state_ref[:, lanes]
        state_low = state.astype(BF16)
        kept_ref[0, :, lanes] = state_low
        mixed = mixed + dot(readout, state_low) * (jnp.exp(wide) * mask[:, 3:4])
        tail = jnp.exp(pair_row(last, first) - wide) * mask[:, 4:5]
        state_ref[:, lanes] = state * pair_row(keep_row, first) + dot(
            inject, (stepped * tail).astype(BF16), 0, 0
        )
        mixed = mixed + wide_ref[0:1, lanes] * feature
        mixed_ref[:, lanes] = mixed
        gate = proj_ref[:, lanes]
        gated = mixed * (gate * sigmoid(gate))
        gated_ref[:, lanes] = gated
        square = square + jnp.sum(gated * gated, axis=1, keepdims=True)
    scale = lax.rsqrt(square * (1.0 / INNER) + 1e-05)
    for pair in range(PAIRS):
        lanes = tile(pair)
        out_ref[:, lanes] = (gated_ref[:, lanes] * scale * wide_ref[1:2, lanes]).astype(BF16)


def backward_kernel(
    proj_ref, prev_ref, mask_ref, seg_col_ref, seg_row_ref, conv_ref, head_ref, wide_ref,
    mixed_ref, kept_ref, grad_ref,
    gproj_ref, gconv_ref, gwide_ref, ghead_ref,
    dstate_ref, shift_ref, carry_ref, back_ref,
):
    @pl.when((pl.program_id(0) == 0) & (pl.program_id(1) == 0))
    def _():
        gconv_ref[...] = jnp.zeros_like(gconv_ref)
        gwide_ref[...] = jnp.zeros_like(gwide_ref)
        ghead_ref[...] = jnp.zeros_like(ghead_ref)

    @pl.when(pl.program_id(1) == 0)
    def _():
        dstate_ref[...] = jnp.zeros_like(dstate_ref)
        carry_ref[...] = jnp.zeros_like(carry_ref)

    load_shift(proj_ref, prev_ref, shift_ref)
    mask = mask_ref[...]
    raw, step, log_decay, cumulated, rows, cols = decays(proj_ref, head_ref)
    turned = cumulated.T
    last = cumulated[CHUNK - 1 : CHUNK, :]
    keep_row = jnp.exp(last) * mask[CHUNK - 1 : CHUNK, 5:6]
    same = (rows >= cols) & (seg_col_ref[...] == seg_row_ref[0])
    bias = jnp.where(same, 0.0, -1e30)
    bias_twice = jnp.concatenate([bias, bias], axis=1)
    summed_inject = conv_tile(proj_ref, shift_ref, conv_ref, mask, PAIRS)
    inject = (summed_inject * sigmoid(summed_inject)).astype(BF16)
    summed_readout = conv_tile(proj_ref, shift_ref, conv_ref, mask, PAIRS + 1)
    readout = (summed_readout * sigmoid(summed_readout)).astype(BF16)
    scores = dot(readout, inject, 1, 1)
    scores_twice = jnp.concatenate([scores, scores], axis=1)

    square = jnp.zeros((CHUNK, 1), F32)
    along = jnp.zeros((CHUNK, 1), F32)
    for pair in range(PAIRS):
        lanes = tile(pair)
        gate = proj_ref[:, lanes]
        gated = mixed_ref[:, lanes] * (gate * sigmoid(gate))
        square = square + jnp.sum(gated * gated, axis=1, keepdims=True)
        along = along + jnp.sum(
            gated * grad_ref[:, lanes] * wide_ref[1:2, lanes], axis=1, keepdims=True
        )
    scale = lax.rsqrt(square * (1.0 / INNER) + 1e-05)
    pull = scale * scale * scale * along * (1.0 / INNER)

    pair_at = lax.broadcasted_iota(jnp.int32, (LANES, LANES), 0) // HEADDIM
    head_at = lax.broadcasted_iota(jnp.int32, (LANES, LANES), 1)
    grad_scores = jnp.zeros((CHUNK, 2 * CHUNK), F32)
    grad_inject = jnp.zeros((CHUNK, STATE), F32)
    grad_readout = jnp.zeros((CHUNK, STATE), F32)
    grad_cumulated = jnp.zeros((CHUNK, LANES), F32)
    grad_step = jnp.zeros((CHUNK, LANES), F32)
    grad_last = jnp.zeros((8, LANES), F32)

    def to_summed(grad_active, summed):
        slope = sigmoid(summed)
        return grad_active * (slope * (1.0 + summed * (1.0 - slope)))

    def conv_back(index, grad_summed):
        lanes = tile(index)
        at = slice(INNER + index * LANES, INNER + (index + 1) * LANES)
        gconv_ref[4:5, lanes] += jnp.sum(grad_summed, axis=0, keepdims=True)
        gconv_ref[3:4, lanes] += jnp.sum(grad_summed * proj_ref[:, at], axis=0, keepdims=True)
        total = conv_ref[3:4, lanes] * grad_summed
        for back in range(1, KERNEL):
            masked = grad_summed * mask[:, back - 1 : back]
            shifted = shift_ref[EDGE - back : EDGE - back + CHUNK, lanes]
            gconv_ref[3 - back : 4 - back, lanes] += jnp.sum(
                masked * shifted, axis=0, keepdims=True
            )
            slot = (index % 2) * (KERNEL - 1) + back - 1
            back_ref[slot, 0:CHUNK, :] = masked
            back_ref[slot, CHUNK : CHUNK + EDGE, :] = carry_ref[back - 1, :, lanes]
            carry_ref[back - 1, :, lanes] = masked[0:EDGE, :]
            total = total + conv_ref[3 - back : 4 - back, lanes] * (
                back_ref[slot, back : back + CHUNK, :]
            )
        gproj_ref[:, at] = total.astype(BF16)

    for pair in range(PAIRS):
        first = 2 * pair
        lanes = tile(pair)
        gather = (head_at == pair_at + first).astype(BF16)
        gate = proj_ref[:, lanes]
        slope = sigmoid(gate)
        silu_gate = gate * slope
        mixed = mixed_ref[:, lanes]
        gated = mixed * silu_gate
        grad_out = grad_ref[:, lanes]
        gwide_ref[1:2, lanes] += jnp.sum(grad_out * gated * scale, axis=0, keepdims=True)
        grad_gated = grad_out * wide_ref[1:2, lanes] * scale - gated * pull
        gproj_ref[:, lanes] = (
            grad_gated * mixed * (slope * (1.0 + gate * (1.0 - slope)))
        ).astype(BF16)
        grad_mixed = grad_gated * silu_gate

        summed = conv_tile(proj_ref, shift_ref, conv_ref, mask, pair)
        feature = summed * sigmoid(summed)
        gwide_ref[0:1, lanes] += jnp.sum(grad_mixed * feature, axis=0, keepdims=True)
        wide_step = halves(spread_column(step, first), spread_column(step, first + 1))
        stepped = feature * wide_step
        stepped_low = stepped.astype(BF16)
        stacked = stack_pair(stepped_low)
        within, wide = pair_decay(cumulated, turned, bias_twice, first)
        mixing = (within * scores_twice).astype(BF16)
        grad_low = grad_mixed.astype(BF16)
        both = dot(mixing, grad_low, 0, 0)
        grad_stepped = halves(both[0:CHUNK, :], both[CHUNK : 2 * CHUNK, :])
        grad_scores = grad_scores + dot(grad_low, stacked, 1, 1) * within
        state_low = kept_ref[0, :, lanes]
        carried = (grad_mixed * (jnp.exp(wide) * mask[:, 3:4])).astype(BF16)
        grad_readout = grad_readout + dot(carried, state_low, 1, 1)
        dstate = dstate_ref[:, lanes]
        dstate_low = dstate.astype(BF16)
        tail = jnp.exp(pair_row(last, first) - wide) * mask[:, 4:5]
        grad_tail = dot(inject, dstate_low) * tail
        grad_inject = grad_inject + dot((stepped * tail).astype(BF16), dstate_low, 1, 1)
        kept_dstate = dstate * pair_row(keep_row, first)
        dstate_ref[:, lanes] = kept_dstate + dot(readout, carried, 0, 0)
        tail_sum = jnp.sum(stepped * grad_tail, axis=0, keepdims=True) + jnp.sum(
            kept_dstate * state_low.astype(F32), axis=0, keepdims=True
        )
        tail_sum = jnp.broadcast_to(tail_sum, (8, LANES))
        tail_high = tail_sum.astype(BF16)
        tail_rest = (tail_sum - tail_high.astype(F32)).astype(BF16)
        grad_last = grad_last + dot(tail_high, gather) + dot(tail_rest, gather)
        flow = (
            grad_low.astype(F32) * (mixed - wide_ref[0:1, lanes] * feature)
            - stepped_low.astype(F32) * grad_stepped
            - stepped * grad_tail
        )
        flow_high = flow.astype(BF16)
        flow_rest = (flow - flow_high.astype(F32)).astype(BF16)
        grad_cumulated = grad_cumulated + dot(
            jnp.concatenate([flow_high, flow_rest], axis=1),
            jnp.concatenate([gather, gather], axis=0),
        )
        grad_stepped = grad_stepped + grad_tail
        grad_step = grad_step + dot((grad_stepped * feature).astype(BF16), gather)
        grad_feature = grad_stepped * wide_step + wide_ref[0:1, lanes] * grad_mixed
        conv_back(pair, to_summed(grad_feature, summed))

    grad_scores = (grad_scores[:, 0:CHUNK] + grad_scores[:, CHUNK : 2 * CHUNK]).astype(BF16)
    grad_readout = grad_readout + dot(grad_scores, inject)
    grad_inject = grad_inject + dot(grad_scores, readout, 0, 0)
    conv_back(PAIRS, to_summed(grad_inject, summed_inject))
    conv_back(PAIRS + 1, to_summed(grad_readout, summed_readout))

    upper = (rows <= cols).astype(F32)
    grad_log = exact_dot(upper, grad_cumulated) + grad_last[0:1, :]
    grad_step = grad_step - head_ref[1:2, :] * grad_log
    lane = lax.broadcasted_iota(jnp.int32, (1, LANES), 1)
    grad_raw = jnp.where(lane < HEADS, grad_step * sigmoid(raw), 0.0)
    gproj_ref[:, STEP_AT:PROJ_PAD] = grad_raw.astype(BF16)
    ghead_ref[0:1, :] += jnp.sum(grad_raw, axis=0, keepdims=True)
    ghead_ref[1:2, :] += jnp.sum(grad_log * log_decay, axis=0, keepdims=True)


def row_specs(order):
    def block(width):
        return pl.BlockSpec((CHUNK, width), lambda m, c: (order(m, c), 0))

    def whole(rows, width):
        return pl.BlockSpec((rows, width), lambda m, c: (0, 0))

    per_edge = CHUNK // EDGE
    common = [
        block(PROJ_PAD),
        pl.BlockSpec(
            (EDGE, PROJ_PAD), lambda m, c: (jnp.maximum(order(m, c) * per_edge - 1, 0), 0)
        ),
        block(8),
        block(1),
        pl.BlockSpec((1, 1, CHUNK), lambda m, c: (order(m, c), 0, 0)),
        whole(8, CONVCH),
        whole(8, LANES),
        whole(8, INNER),
    ]
    state = pl.BlockSpec((1, STATE, INNER), lambda m, c: (order(m, c), 0, 0))
    return common, block, whole, state


def mixer_forward(operands):
    count = operands[0].shape[0]
    common, block, whole, state = row_specs(lambda m, c: m * CHUNKS + c)
    return pl.pallas_call(
        forward_kernel,
        grid=(count // MB_TOK, CHUNKS),
        in_specs=common,
        out_specs=[block(INNER), block(INNER), state],
        out_shape=[
            jax.ShapeDtypeStruct((count, INNER), BF16),
            jax.ShapeDtypeStruct((count, INNER), F32),
            jax.ShapeDtypeStruct((count // CHUNK, STATE, INNER), BF16),
        ],
        scratch_shapes=[
            pltpu.VMEM((STATE, INNER), F32),
            pltpu.VMEM((EDGE + CHUNK, CONVCH), F32),
            pltpu.VMEM((CHUNK, INNER), F32),
        ],
        compiler_params=pltpu.CompilerParams(vmem_limit_bytes=48 * 1024 * 1024),
        cost_estimate=pl.CostEstimate(
            flops=count * INNER * 2000, bytes_accessed=count * INNER * 20, transcendentals=0
        ),
        name="mixer_forward",
    )(*operands)


def mixer_backward(operands, mixed, kept, grad_mixer):
    count = operands[0].shape[0]
    common, block, whole, state = row_specs(lambda m, c: m * CHUNKS + CHUNKS - 1 - c)
    return pl.pallas_call(
        backward_kernel,
        grid=(count // MB_TOK, CHUNKS),
        in_specs=common + [block(INNER), state, block(INNER)],
        out_specs=[block(PROJ_PAD), whole(8, CONVCH), whole(8, INNER), whole(8, LANES)],
        out_shape=[
            jax.ShapeDtypeStruct((count, PROJ_PAD), BF16),
            jax.ShapeDtypeStruct((8, CONVCH), F32),
            jax.ShapeDtypeStruct((8, INNER), F32),
            jax.ShapeDtypeStruct((8, LANES), F32),
        ],
        scratch_shapes=[
            pltpu.VMEM((STATE, INNER), F32),
            pltpu.VMEM((EDGE + CHUNK, CONVCH), F32),
            pltpu.VMEM((KERNEL - 1, EDGE, CONVCH), F32),
            pltpu.VMEM((2 * (KERNEL - 1), CHUNK + EDGE, LANES), F32),
        ],
        compiler_params=pltpu.CompilerParams(vmem_limit_bytes=48 * 1024 * 1024),
        cost_estimate=pl.CostEstimate(
            flops=count * INNER * 6000, bytes_accessed=count * INNER * 30, transcendentals=0
        ),
        name="mixer_backward",
    )(*operands, mixed, kept, grad_mixer)


def segment_masks(segments):
    blocks = segments.reshape(-1, MB_TOK)
    columns = []
    for back in range(1, KERNEL):
        prior = jnp.pad(blocks, ((0, 0), (back, 0)), constant_values=-2)[:, :MB_TOK]
        columns.append((prior == blocks).reshape(-1))
    chunks = blocks.reshape(-1, CHUNKS, CHUNK)
    final = chunks[:, :, CHUNK - 1]
    before = jnp.pad(final, ((0, 0), (1, 0)), constant_values=-2)[:, :CHUNKS]
    columns.append((chunks == before[:, :, None]).reshape(-1))
    columns.append((chunks == final[:, :, None]).reshape(-1))
    columns.append(jnp.broadcast_to((final == before)[:, :, None], chunks.shape).reshape(-1))
    columns.extend([jnp.zeros_like(columns[0])] * 2)
    return jnp.stack(columns, axis=1).astype(F32)


def layout_shapes():
    return [
        (D,),
        (D, PROJ),
        (KERNEL, CONVCH),
        (CONVCH,),
        (HEADS,),
        (HEADS,),
        (HEADS,),
        (INNER,),
        (INNER, D),
    ]


def unpack(flat_weights):
    pieces = []
    offset = 0
    for piece_shape in layout_shapes():
        amount = math.prod(piece_shape)
        pieces.append(flat_weights[offset : offset + amount].reshape(piece_shape))
        offset = offset + amount
    return pieces


def rms_scale(values):
    return values * lax.rsqrt(jnp.mean(values * values, axis=-1, keepdims=True) + 1e-05)


def norm_gain(values, gains):
    return rms_scale(values) * gains


def layer_weights(flat_weights):
    pieces = unpack(flat_weights)
    in_weight = jnp.pad(pieces[1], ((0, 0), (0, PROJ_PAD - PROJ)))
    small = [piece.astype(F32) for piece in pieces[2:8]]
    conv = jnp.concatenate([small[0], small[1][None], jnp.zeros((3, CONVCH), F32)])
    head = jnp.pad(
        jnp.stack([small[2], jnp.exp(small[3])]), ((0, 6), (0, LANES - HEADS))
    )
    wide = jnp.concatenate(
        [jnp.repeat(small[4], HEADDIM)[None], small[5][None], jnp.zeros((6, INNER), F32)]
    )
    return pieces[0].astype(F32), in_weight, (conv, head, wide), pieces[8]


def per_device(tokens, params, segments, cotangent):
    count = tokens.shape[0]
    devices = lax.axis_size("dp")
    shard = params.shape[1]
    padded_shard = -(-shard // 2048) * 2048
    live = (segments >= 0).astype(F32)[:, None]
    masks = segment_masks(segments)
    seg_col = segments[:, None]
    seg_row = segments.reshape(-1, 1, CHUNK)
    weights = []
    for layer in range(LAYERS):
        mine = jnp.pad(params[layer], (0, padded_shard - shard))
        flat = lax.all_gather(mine, "dp", axis=0)[:, :shard].reshape(-1)
        weights.append(layer_weights(flat))
    stream = tokens.astype(F32)
    records = []
    for layer in range(LAYERS):
        in_gain, in_weight, small, out_weight = weights[layer]
        normed_value, norm_pull = jax.vjp(norm_gain, stream, in_gain)
        normed = normed_value.astype(BF16)
        projected = dot(normed, in_weight)
        operands = (projected, projected, masks, seg_col, seg_row) + small
        mixer_out, mixed, kept = mixer_forward(operands)
        stream = stream + dot(mixer_out, out_weight) * live
        records.append((normed, norm_pull, operands, mixer_out, mixed, kept))
    out_tokens = stream.astype(BF16)
    grad_stream = cotangent.astype(F32)
    shards = [None] * LAYERS
    for layer in reversed(range(LAYERS)):
        in_gain, in_weight, small, out_weight = weights[layer]
        normed, norm_pull, operands, mixer_out, mixed, kept = records[layer]
        branch = (grad_stream * live).astype(BF16)
        grad_out_weight = dot(mixer_out, branch, 0, 0)
        grad_mixer = dot(branch, out_weight, 1, 1)
        grad_projected, gconv, gwide, ghead = mixer_backward(operands, mixed, kept, grad_mixer)
        grad_in_weight = dot(normed, grad_projected, 0, 0)[:, :PROJ]
        grad_normed = dot(grad_projected, in_weight, 1, 1)
        stream_part, gain_grad = norm_pull(grad_normed)
        grad_stream = grad_stream + stream_part
        members = [
            gain_grad,
            grad_in_weight,
            gconv[:4],
            gconv[4],
            ghead[0, :HEADS],
            ghead[1, :HEADS],
            gwide[0].reshape(HEADS, HEADDIM).sum(axis=1),
            gwide[1],
            grad_out_weight,
            jnp.zeros((shard * devices - PARAMS,), F32),
        ]
        flat = jnp.concatenate([member.reshape(-1) for member in members])
        rows = jnp.pad(flat.reshape(devices, shard), ((0, 0), (0, padded_shard - shard)))
        rows = rows.reshape(-1, LANES)
        if layer + 1 < LAYERS:
            rows, shards[layer + 1] = lax.optimization_barrier((rows, shards[layer + 1]))
        summed = lax.psum_scatter(rows, "dp", scatter_dimension=0, tiled=True)
        shards[layer] = summed.reshape(-1)[:shard]
    return out_tokens, grad_stream, jnp.stack(shards)


def solution(mesh):
    in_specs = (P("dp", None), P(None, "dp"), P("dp"), P("dp", None))
    out_specs = (P("dp", None), P("dp", None), P(None, "dp"))
    return jax.shard_map(
        per_device, mesh=mesh, in_specs=in_specs, out_specs=out_specs, check_vma=False
    )
```

```python
import math

import jax
import jax.numpy as jnp
from jax import lax
from jax.experimental import pallas as pl
from jax.experimental.pallas import tpu as pltpu
from jax.sharding import PartitionSpec as P

D = 768
INNER = 1536
HEADDIM = 64
STATE = 128
KERNEL = 4
MB_TOK = 1024
LAYERS = 2
HEADS = 24
CONVCH = 1792
PROJ = 3352
PARAMS = 3765320

LANES = 128
CHUNK = 128
CHUNKS = MB_TOK // CHUNK
PAIRS = HEADS // 2
PROJ_PAD = INNER + CONVCH + LANES
STEP_AT = INNER + CONVCH
TILES = CONVCH // LANES
EDGE = 8
F32 = jnp.float32
BF16 = jnp.bfloat16
highest = lax.Precision.HIGHEST


def tile(index):
    return slice(index * LANES, (index + 1) * LANES)


def dot(left, right, left_dim=1, right_dim=0):
    return lax.dot_general(
        left, right, (((left_dim,), (right_dim,)), ((), ())), preferred_element_type=F32
    )


def exact_dot(left, right):
    return jnp.dot(left, right, preferred_element_type=F32, precision=highest)


def sigmoid(values):
    return 1.0 / (1.0 + jnp.exp(-values))


def softplus(values):
    return jnp.maximum(values, 0.0) + jnp.log1p(jnp.exp(-jnp.abs(values)))


def halves(first, second):
    lane = lax.broadcasted_iota(jnp.int32, (1, LANES), 1)
    return jnp.where(lane < HEADDIM, first, second)


def spread_column(values, index):
    return jnp.broadcast_to(values[:, index : index + 1], (CHUNK, LANES))


def conv_tile(proj_ref, shift_ref, conv_ref, mask, index):
    at = slice(INNER + index * LANES, INNER + (index + 1) * LANES)
    lanes = tile(index)
    total = conv_ref[4:5, lanes] + conv_ref[3:4, lanes] * proj_ref[:, at]
    for back in range(1, KERNEL):
        shifted = shift_ref[EDGE - back : EDGE - back + CHUNK, lanes]
        total = total + conv_ref[3 - back : 4 - back, lanes] * shifted * mask[:, back - 1 : back]
    return total


def load_shift(proj_ref, prev_ref, shift_ref):
    shift_ref[0:EDGE, :] = prev_ref[:, INNER:STEP_AT]
    shift_ref[EDGE : EDGE + CHUNK, :] = proj_ref[:, INNER:STEP_AT]


def decays(proj_ref, head_ref):
    raw = proj_ref[:, STEP_AT:PROJ_PAD] + head_ref[0:1, :]
    step = softplus(raw)
    log_decay = -head_ref[1:2, :] * step
    rows = lax.broadcasted_iota(jnp.int32, (CHUNK, CHUNK), 0)
    cols = lax.broadcasted_iota(jnp.int32, (CHUNK, CHUNK), 1)
    lower = (rows >= cols).astype(F32)
    cumulated = exact_dot(lower, log_decay)
    return raw, step, log_decay, cumulated, rows, cols


def pair_decay(cumulated, turned, bias_twice, first):
    wide_a = spread_column(cumulated, first)
    wide_b = spread_column(cumulated, first + 1)
    row = jnp.concatenate([turned[first : first + 1, :], turned[first + 1 : first + 2, :]], axis=1)
    within = jnp.exp(jnp.concatenate([wide_a, wide_b], axis=1) - row + bias_twice)
    return within, halves(wide_a, wide_b)


def stack_pair(values):
    zero = jnp.zeros_like(values)
    return jnp.concatenate([halves(values, zero), halves(zero, values)], axis=0)


def pair_row(row, first):
    return halves(row[:, first : first + 1], row[:, first + 1 : first + 2])


def forward_kernel(
    proj_ref, prev_ref, mask_ref, seg_col_ref, seg_row_ref, conv_ref, head_ref, wide_ref,
    out_ref, mixed_ref, kept_ref, state_ref, shift_ref, gated_ref,
):
    @pl.when(pl.program_id(1) == 0)
    def _():
        state_ref[...] = jnp.zeros_like(state_ref)

    load_shift(proj_ref, prev_ref, shift_ref)
    mask = mask_ref[...]
    raw, step, log_decay, cumulated, rows, cols = decays(proj_ref, head_ref)
    turned = cumulated.T
    last = cumulated[CHUNK - 1 : CHUNK, :]
    keep_row = jnp.exp(last) * mask[CHUNK - 1 : CHUNK, 5:6]
    same = (rows >= cols) & (seg_col_ref[...] == seg_row_ref[0])
    bias = jnp.where(same, 0.0, -1e30)
    bias_twice = jnp.concatenate([bias, bias], axis=1)
    summed = conv_tile(proj_ref, shift_ref, conv_ref, mask, PAIRS)
    inject = (summed * sigmoid(summed)).astype(BF16)
    summed = conv_tile(proj_ref, shift_ref, conv_ref, mask, PAIRS + 1)
    readout = (summed * sigmoid(summed)).astype(BF16)
    scores = dot(readout, inject, 1, 1)
    scores_twice = jnp.concatenate([scores, scores], axis=1)
    square = jnp.zeros((CHUNK, 1), F32)
    for pair in range(PAIRS):
        first = 2 * pair
        lanes = tile(pair)
        summed = conv_tile(proj_ref, shift_ref, conv_ref, mask, pair)
        feature = summed * sigmoid(summed)
        stepped = feature * halves(spread_column(step, first), spread_column(step, first + 1))
        within, wide = pair_decay(cumulated, turned, bias_twice, first)
        mixing = (within * scores_twice).astype(BF16)
        mixed = dot(mixing, stack_pair(stepped.astype(BF16)))
        state = state_ref[:, lanes]
        state_low = state.astype(BF16)
        kept_ref[0, :, lanes] = state_low
        mixed = mixed + dot(readout, state_low) * (jnp.exp(wide) * mask[:, 3:4])
        tail = jnp.exp(pair_row(last, first) - wide) * mask[:, 4:5]
        state_ref[:, lanes] = state * pair_row(keep_row, first) + dot(
            inject, (stepped * tail).astype(BF16), 0, 0
        )
        mixed = mixed + wide_ref[0:1, lanes] * feature
        mixed_ref[:, lanes] = mixed
        gate = proj_ref[:, lanes]
        gated = mixed * (gate * sigmoid(gate))
        gated_ref[:, lanes] = gated
        square = square + jnp.sum(gated * gated, axis=1, keepdims=True)
    scale = lax.rsqrt(square * (1.0 / INNER) + 1e-05)
    for pair in range(PAIRS):
        lanes = tile(pair)
        out_ref[:, lanes] = (gated_ref[:, lanes] * scale * wide_ref[1:2, lanes]).astype(BF16)


def backward_kernel(
    proj_ref, prev_ref, mask_ref, seg_col_ref, seg_row_ref, conv_ref, head_ref, wide_ref,
    mixed_ref, kept_ref, grad_ref,
    gproj_ref, gconv_ref, gwide_ref, ghead_ref,
    dstate_ref, shift_ref, carry_ref, back_ref,
):
    @pl.when((pl.program_id(0) == 0) & (pl.program_id(1) == 0))
    def _():
        gconv_ref[...] = jnp.zeros_like(gconv_ref)
        gwide_ref[...] = jnp.zeros_like(gwide_ref)
        ghead_ref[...] = jnp.zeros_like(ghead_ref)

    @pl.when(pl.program_id(1) == 0)
    def _():
        dstate_ref[...] = jnp.zeros_like(dstate_ref)
        carry_ref[...] = jnp.zeros_like(carry_ref)

    load_shift(proj_ref, prev_ref, shift_ref)
    mask = mask_ref[...]
    raw, step, log_decay, cumulated, rows, cols = decays(proj_ref, head_ref)
    turned = cumulated.T
    last = cumulated[CHUNK - 1 : CHUNK, :]
    keep_row = jnp.exp(last) * mask[CHUNK - 1 : CHUNK, 5:6]
    same = (rows >= cols) & (seg_col_ref[...] == seg_row_ref[0])
    bias = jnp.where(same, 0.0, -1e30)
    bias_twice = jnp.concatenate([bias, bias], axis=1)
    summed_inject = conv_tile(proj_ref, shift_ref, conv_ref, mask, PAIRS)
    inject = (summed_inject * sigmoid(summed_inject)).astype(BF16)
    summed_readout = conv_tile(proj_ref, shift_ref, conv_ref, mask, PAIRS + 1)
    readout = (summed_readout * sigmoid(summed_readout)).astype(BF16)
    scores = dot(readout, inject, 1, 1)
    scores_twice = jnp.concatenate([scores, scores], axis=1)

    square = jnp.zeros((CHUNK, 1), F32)
    along = jnp.zeros((CHUNK, 1), F32)
    for pair in range(PAIRS):
        lanes = tile(pair)
        gate = proj_ref[:, lanes]
        gated = mixed_ref[:, lanes] * (gate * sigmoid(gate))
        square = square + jnp.sum(gated * gated, axis=1, keepdims=True)
        along = along + jnp.sum(
            gated * grad_ref[:, lanes] * wide_ref[1:2, lanes], axis=1, keepdims=True
        )
    scale = lax.rsqrt(square * (1.0 / INNER) + 1e-05)
    pull = scale * scale * scale * along * (1.0 / INNER)

    pair_at = lax.broadcasted_iota(jnp.int32, (LANES, LANES), 0) // HEADDIM
    head_at = lax.broadcasted_iota(jnp.int32, (LANES, LANES), 1)
    grad_scores = jnp.zeros((CHUNK, 2 * CHUNK), F32)
    grad_inject = jnp.zeros((CHUNK, STATE), F32)
    grad_readout = jnp.zeros((CHUNK, STATE), F32)
    grad_cumulated = jnp.zeros((CHUNK, LANES), F32)
    grad_step = jnp.zeros((CHUNK, LANES), F32)
    grad_last = jnp.zeros((8, LANES), F32)

    def to_summed(grad_active, summed):
        slope = sigmoid(summed)
        return grad_active * (slope * (1.0 + summed * (1.0 - slope)))

    def conv_back(index, grad_summed):
        lanes = tile(index)
        at = slice(INNER + index * LANES, INNER + (index + 1) * LANES)
        gconv_ref[4:5, lanes] += jnp.sum(grad_summed, axis=0, keepdims=True)
        gconv_ref[3:4, lanes] += jnp.sum(grad_summed * proj_ref[:, at], axis=0, keepdims=True)
        total = conv_ref[3:4, lanes] * grad_summed
        for back in range(1, KERNEL):
            masked = grad_summed * mask[:, back - 1 : back]
            shifted = shift_ref[EDGE - back : EDGE - back + CHUNK, lanes]
            gconv_ref[3 - back : 4 - back, lanes] += jnp.sum(
                masked * shifted, axis=0, keepdims=True
            )
            slot = (index % 2) * (KERNEL - 1) + back - 1
            back_ref[slot, 0:CHUNK, :] = masked
            back_ref[slot, CHUNK : CHUNK + EDGE, :] = carry_ref[back - 1, :, lanes]
            carry_ref[back - 1, :, lanes] = masked[0:EDGE, :]
            total = total + conv_ref[3 - back : 4 - back, lanes] * (
                back_ref[slot, back : back + CHUNK, :]
            )
        gproj_ref[:, at] = total.astype(BF16)

    for pair in range(PAIRS):
        first = 2 * pair
        lanes = tile(pair)
        gather = (head_at == pair_at + first).astype(BF16)
        gate = proj_ref[:, lanes]
        slope = sigmoid(gate)
        silu_gate = gate * slope
        mixed = mixed_ref[:, lanes]
        gated = mixed * silu_gate
        grad_out = grad_ref[:, lanes]
        gwide_ref[1:2, lanes] += jnp.sum(grad_out * gated * scale, axis=0, keepdims=True)
        grad_gated = grad_out * wide_ref[1:2, lanes] * scale - gated * pull
        gproj_ref[:, lanes] = (
            grad_gated * mixed * (slope * (1.0 + gate * (1.0 - slope)))
        ).astype(BF16)
        grad_mixed = grad_gated * silu_gate

        summed = conv_tile(proj_ref, shift_ref, conv_ref, mask, pair)
        feature = summed * sigmoid(summed)
        gwide_ref[0:1, lanes] += jnp.sum(grad_mixed * feature, axis=0, keepdims=True)
        wide_step = halves(spread_column(step, first), spread_column(step, first + 1))
        stepped = feature * wide_step
        stepped_low = stepped.astype(BF16)
        stacked = stack_pair(stepped_low)
        within, wide = pair_decay(cumulated, turned, bias_twice, first)
        mixing = (within * scores_twice).astype(BF16)
        grad_low = grad_mixed.astype(BF16)
        both = dot(mixing, grad_low, 0, 0)
        grad_stepped = halves(both[0:CHUNK, :], both[CHUNK : 2 * CHUNK, :])
        grad_scores = grad_scores + dot(grad_low, stacked, 1, 1) * within
        state_low = kept_ref[0, :, lanes]
        carried = (grad_mixed * (jnp.exp(wide) * mask[:, 3:4])).astype(BF16)
        grad_readout = grad_readout + dot(carried, state_low, 1, 1)
        dstate = dstate_ref[:, lanes]
        dstate_low = dstate.astype(BF16)
        tail = jnp.exp(pair_row(last, first) - wide) * mask[:, 4:5]
        grad_tail = dot(inject, dstate_low) * tail
        grad_inject = grad_inject + dot((stepped * tail).astype(BF16), dstate_low, 1, 1)
        kept_dstate = dstate * pair_row(keep_row, first)
        dstate_ref[:, lanes] = kept_dstate + dot(readout, carried, 0, 0)
        tail_sum = jnp.sum(stepped * grad_tail, axis=0, keepdims=True) + jnp.sum(
            kept_dstate * state_low.astype(F32), axis=0, keepdims=True
        )
        tail_sum = jnp.broadcast_to(tail_sum, (8, LANES))
        tail_high = tail_sum.astype(BF16)
        tail_rest = (tail_sum - tail_high.astype(F32)).astype(BF16)
        grad_last = grad_last + dot(tail_high, gather) + dot(tail_rest, gather)
        flow = (
            grad_low.astype(F32) * (mixed - wide_ref[0:1, lanes] * feature)
            - stepped_low.astype(F32) * grad_stepped
            - stepped * grad_tail
        )
        flow_high = flow.astype(BF16)
        flow_rest = (flow - flow_high.astype(F32)).astype(BF16)
        grad_cumulated = grad_cumulated + dot(
            jnp.concatenate([flow_high, flow_rest], axis=1),
            jnp.concatenate([gather, gather], axis=0),
        )
        grad_stepped = grad_stepped + grad_tail
        grad_step = grad_step + dot((grad_stepped * feature).astype(BF16), gather)
        grad_feature = grad_stepped * wide_step + wide_ref[0:1, lanes] * grad_mixed
        conv_back(pair, to_summed(grad_feature, summed))

    grad_scores = (grad_scores[:, 0:CHUNK] + grad_scores[:, CHUNK : 2 * CHUNK]).astype(BF16)
    grad_readout = grad_readout + dot(grad_scores, inject)
    grad_inject = grad_inject + dot(grad_scores, readout, 0, 0)
    conv_back(PAIRS, to_summed(grad_inject, summed_inject))
    conv_back(PAIRS + 1, to_summed(grad_readout, summed_readout))

    upper = (rows <= cols).astype(F32)
    grad_log = exact_dot(upper, grad_cumulated) + grad_last[0:1, :]
    grad_step = grad_step - head_ref[1:2, :] * grad_log
    lane = lax.broadcasted_iota(jnp.int32, (1, LANES), 1)
    grad_raw = jnp.where(lane < HEADS, grad_step * sigmoid(raw), 0.0)
    gproj_ref[:, STEP_AT:PROJ_PAD] = grad_raw.astype(BF16)
    ghead_ref[0:1, :] += jnp.sum(grad_raw, axis=0, keepdims=True)
    ghead_ref[1:2, :] += jnp.sum(grad_log * log_decay, axis=0, keepdims=True)


def row_specs(order):
    def block(width):
        return pl.BlockSpec((CHUNK, width), lambda m, c: (order(m, c), 0))

    def whole(rows, width):
        return pl.BlockSpec((rows, width), lambda m, c: (0, 0))

    per_edge = CHUNK // EDGE
    common = [
        block(PROJ_PAD),
        pl.BlockSpec(
            (EDGE, PROJ_PAD), lambda m, c: (jnp.maximum(order(m, c) * per_edge - 1, 0), 0)
        ),
        block(8),
        block(1),
        pl.BlockSpec((1, 1, CHUNK), lambda m, c: (order(m, c), 0, 0)),
        whole(8, CONVCH),
        whole(8, LANES),
        whole(8, INNER),
    ]
    state = pl.BlockSpec((1, STATE, INNER), lambda m, c: (order(m, c), 0, 0))
    return common, block, whole, state


def mixer_forward(operands):
    count = operands[0].shape[0]
    common, block, whole, state = row_specs(lambda m, c: m * CHUNKS + c)
    return pl.pallas_call(
        forward_kernel,
        grid=(count // MB_TOK, CHUNKS),
        in_specs=common,
        out_specs=[block(INNER), block(INNER), state],
        out_shape=[
            jax.ShapeDtypeStruct((count, INNER), BF16),
            jax.ShapeDtypeStruct((count, INNER), F32),
            jax.ShapeDtypeStruct((count // CHUNK, STATE, INNER), BF16),
        ],
        scratch_shapes=[
            pltpu.VMEM((STATE, INNER), F32),
            pltpu.VMEM((EDGE + CHUNK, CONVCH), F32),
            pltpu.VMEM((CHUNK, INNER), F32),
        ],
        compiler_params=pltpu.CompilerParams(vmem_limit_bytes=48 * 1024 * 1024),
        cost_estimate=pl.CostEstimate(
            flops=count * INNER * 2000, bytes_accessed=count * INNER * 20, transcendentals=0
        ),
        name="mixer_forward",
    )(*operands)


def mixer_backward(operands, mixed, kept, grad_mixer):
    count = operands[0].shape[0]
    common, block, whole, state = row_specs(lambda m, c: m * CHUNKS + CHUNKS - 1 - c)
    return pl.pallas_call(
        backward_kernel,
        grid=(count // MB_TOK, CHUNKS),
        in_specs=common + [block(INNER), state, block(INNER)],
        out_specs=[block(PROJ_PAD), whole(8, CONVCH), whole(8, INNER), whole(8, LANES)],
        out_shape=[
            jax.ShapeDtypeStruct((count, PROJ_PAD), BF16),
            jax.ShapeDtypeStruct((8, CONVCH), F32),
            jax.ShapeDtypeStruct((8, INNER), F32),
            jax.ShapeDtypeStruct((8, LANES), F32),
        ],
        scratch_shapes=[
            pltpu.VMEM((STATE, INNER), F32),
            pltpu.VMEM((EDGE + CHUNK, CONVCH), F32),
            pltpu.VMEM((KERNEL - 1, EDGE, CONVCH), F32),
            pltpu.VMEM((2 * (KERNEL - 1), CHUNK + EDGE, LANES), F32),
        ],
        compiler_params=pltpu.CompilerParams(vmem_limit_bytes=48 * 1024 * 1024),
        cost_estimate=pl.CostEstimate(
            flops=count * INNER * 6000, bytes_accessed=count * INNER * 30, transcendentals=0
        ),
        name="mixer_backward",
    )(*operands, mixed, kept, grad_mixer)


def segment_masks(segments):
    blocks = segments.reshape(-1, MB_TOK)
    columns = []
    for back in range(1, KERNEL):
        prior = jnp.pad(blocks, ((0, 0), (back, 0)), constant_values=-2)[:, :MB_TOK]
        columns.append((prior == blocks).reshape(-1))
    chunks = blocks.reshape(-1, CHUNKS, CHUNK)
    final = chunks[:, :, CHUNK - 1]
    before = jnp.pad(final, ((0, 0), (1, 0)), constant_values=-2)[:, :CHUNKS]
    columns.append((chunks == before[:, :, None]).reshape(-1))
    columns.append((chunks == final[:, :, None]).reshape(-1))
    columns.append(jnp.broadcast_to((final == before)[:, :, None], chunks.shape).reshape(-1))
    columns.extend([jnp.zeros_like(columns[0])] * 2)
    return jnp.stack(columns, axis=1).astype(F32)


def layout_shapes():
    return [
        (D,),
        (D, PROJ),
        (KERNEL, CONVCH),
        (CONVCH,),
        (HEADS,),
        (HEADS,),
        (HEADS,),
        (INNER,),
        (INNER, D),
    ]


def unpack(flat_weights):
    pieces = []
    offset = 0
    for piece_shape in layout_shapes():
        amount = math.prod(piece_shape)
        pieces.append(flat_weights[offset : offset + amount].reshape(piece_shape))
        offset = offset + amount
    return pieces


def rms_scale(values):
    return values * lax.rsqrt(jnp.mean(values * values, axis=-1, keepdims=True) + 1e-05)


def norm_gain(values, gains):
    return rms_scale(values) * gains


def layer_weights(flat_weights):
    pieces = unpack(flat_weights)
    in_weight = jnp.pad(pieces[1], ((0, 0), (0, PROJ_PAD - PROJ)))
    small = [piece.astype(F32) for piece in pieces[2:8]]
    conv = jnp.concatenate([small[0], small[1][None], jnp.zeros((3, CONVCH), F32)])
    head = jnp.pad(
        jnp.stack([small[2], jnp.exp(small[3])]), ((0, 6), (0, LANES - HEADS))
    )
    wide = jnp.concatenate(
        [jnp.repeat(small[4], HEADDIM)[None], small[5][None], jnp.zeros((6, INNER), F32)]
    )
    return pieces[0].astype(F32), in_weight, (conv, head, wide), pieces[8]


def per_device(tokens, params, segments, cotangent):
    count = tokens.shape[0]
    devices = lax.axis_size("dp")
    shard = params.shape[1]
    padded_shard = -(-shard // 2048) * 2048
    live = (segments >= 0).astype(F32)[:, None]
    masks = segment_masks(segments)
    seg_col = segments[:, None]
    seg_row = segments.reshape(-1, 1, CHUNK)
    weights = []
    for layer in range(LAYERS):
        mine = jnp.pad(params[layer], (0, padded_shard - shard))
        flat = lax.all_gather(mine, "dp", axis=0)[:, :shard].reshape(-1)
        weights.append(layer_weights(flat))
    stream = tokens.astype(F32)
    records = []
    for layer in range(LAYERS):
        in_gain, in_weight, small, out_weight = weights[layer]
        normed_value, norm_pull = jax.vjp(norm_gain, stream, in_gain)
        normed = normed_value.astype(BF16)
        projected = dot(normed, in_weight)
        operands = (projected, projected, masks, seg_col, seg_row) + small
        mixer_out, mixed, kept = mixer_forward(operands)
        stream = stream + dot(mixer_out, out_weight) * live
        records.append((normed, norm_pull, operands, mixer_out, mixed, kept))
    out_tokens = stream.astype(BF16)
    grad_stream = cotangent.astype(F32)
    shards = [None] * LAYERS
    for layer in reversed(range(LAYERS)):
        in_gain, in_weight, small, out_weight = weights[layer]
        normed, norm_pull, operands, mixer_out, mixed, kept = records[layer]
        branch = (grad_stream * live).astype(BF16)
        grad_out_weight = dot(mixer_out, branch, 0, 0)
        grad_mixer = dot(branch, out_weight, 1, 1)
        grad_projected, gconv, gwide, ghead = mixer_backward(operands, mixed, kept, grad_mixer)
        grad_in_weight = dot(normed, grad_projected, 0, 0)[:, :PROJ]
        grad_normed = dot(grad_projected, in_weight, 1, 1)
        stream_part, gain_grad = norm_pull(grad_normed)
        grad_stream = grad_stream + stream_part
        small_grads = jnp.concatenate(
            [
                gconv[:5].reshape(-1),
                ghead[0, :HEADS],
                ghead[1, :HEADS],
                gwide[0].reshape(HEADS, HEADDIM).sum(axis=1),
                gwide[1],
            ]
        )
        flat = jnp.zeros((shard * devices,), F32)
        offset = 0
        for member in (gain_grad, grad_in_weight, small_grads, grad_out_weight):
            spare = shard * devices - offset - member.size
            flat = flat + lax.pad(member.reshape(-1), jnp.float32(0.0), ((offset, spare, 0),))
            offset = offset + member.size
        rows = jnp.pad(flat.reshape(devices, shard), ((0, 0), (0, padded_shard - shard)))
        rows = rows.reshape(-1, LANES)
        if layer + 1 < LAYERS:
            rows, shards[layer + 1] = lax.optimization_barrier((rows, shards[layer + 1]))
        summed = lax.psum_scatter(rows, "dp", scatter_dimension=0, tiled=True)
        shards[layer] = summed.reshape(-1)[:shard]
    return out_tokens, grad_stream, jnp.stack(shards)


def solution(mesh):
    in_specs = (P("dp", None), P(None, "dp"), P("dp"), P("dp", None))
    out_specs = (P("dp", None), P("dp", None), P(None, "dp"))
    return jax.shard_map(
        per_device, mesh=mesh, in_specs=in_specs, out_specs=out_specs, check_vma=False
    )
```
